256 devices in a mesh: dp: 4 (over z_lo), seq: 64 (over y, x, z_hi, core).
Axes of the slice: x: 4, y: 4, z: 8 (z_hi: 2, z_lo: 4; z = z_hi * 4 + z_lo), core: 2. Of those that a mesh axis runs over, the one named last changes fastest.
Arguments:
- grad_out: bfloat16 [4, 8192, 4096], P('dp', 'seq'), may hold values from -6 to 6
- query_proj: bfloat16 [4, 8192, 4096], P('dp', 'seq'), may hold values from -6 to 6
- key_proj: bfloat16 [4, 8192, 4096], P('dp', 'seq'), may hold values from -6 to 6
- value_proj: bfloat16 [4, 8192, 4096], P('dp', 'seq'), may hold values from -6 to 6
- conv_out: bfloat16 [4, 8192, 4096], P('dp', 'seq'), may hold values from -6 to 6
- filters: float32 [4096, 8192], P('seq'), may hold values from -0.0625 to 0.0625
Outputs:
- grad_query: bfloat16 [4, 8192, 4096], P('dp', 'seq')
- grad_key: bfloat16 [4, 8192, 4096], P('dp', 'seq')
- grad_value: bfloat16 [4, 8192, 4096], P('dp', 'seq')
- filter_grad: float32 [4096, 8192], P('seq', 'dp')
The draws below stay inside these ranges and needn't reach their ends.
All inputs are finite; a program needn't handle non-finite values.
Results may differ from the reference program's by a relative error of at most 0.0058.
Values may be sent and summed in bfloat16 or wider, within the bound.
A program may use at most 128 MiB of HBM per device.

```python
import math
import jax
import jax.numpy as jnp
from jax import lax

C = 4096
LENGTH = 8192
BATCH = 4


def block_levels(key, shape, cuts, low, high):
    level, own = 1.0, jax.random.fold_in(key, 6)
    for dim, shards_of in cuts:
        heights = jnp.exp(jax.random.uniform(jax.random.fold_in(own, dim), (shards_of,), jnp.float32, low / len(cuts), high / len(cuts)))
        level = level * jnp.repeat(heights, shape[dim] // shards_of).reshape([-1 if axis == dim else 1 for axis in range(len(shape))])
    return level


def scatter_about(own_key, extent, spread, reach, pieces=(), kind=jnp.bfloat16):
    level = block_levels(own_key, extent, pieces, -0.22, 0.18) if pieces else 1.0
    result = jax.random.normal(own_key, extent, jnp.float32) * spread * level
    return jnp.minimum(jnp.maximum(result, -reach), reach).astype(kind)


def setup_inputs(seed: int = 0) -> dict:
    keys = jax.random.split(jax.random.key(seed), 7)
    return {
        "grad_out": scatter_about(keys[0], (BATCH, LENGTH, C), 1.0, 6.0, ((0, 4), (1, 64))),
        "query_proj": scatter_about(keys[1], (BATCH, LENGTH, C), 1.0, 6.0, ((0, 4), (1, 64))),
        "key_proj": scatter_about(keys[2], (BATCH, LENGTH, C), 1.0, 6.0, ((0, 4), (1, 64))),
        "value_proj": scatter_about(keys[3], (BATCH, LENGTH, C), 1.0, 6.0, ((0, 4), (1, 64))),
        "conv_out": scatter_about(keys[4], (BATCH, LENGTH, C), 1.0, 6.0, ((0, 4), (1, 64))),
        "filters": scatter_about(keys[5], (C, LENGTH), LENGTH ** -0.5, 0.0625, ((0, 64),), jnp.float32),
    }


def reference(grad_out, query_proj, key_proj, value_proj, conv_out, filters):
    size_fft = 2 * LENGTH
    filt_spectrum = jnp.fft.rfft(filters.astype(jnp.float32), n=size_fft, axis=1)

    def one_sequence(inputs):
        grad_seq, query_seq, key_seq, value_seq = inputs
        product = (key_seq.astype(jnp.float32) * value_seq.astype(jnp.float32)).astype(jnp.bfloat16)
        signal = (grad_seq.astype(jnp.float32) * query_seq.astype(jnp.float32)).astype(jnp.bfloat16)
        prod_spectrum = jnp.fft.rfft(product.astype(jnp.float32).T, n=size_fft, axis=1)
        sig_spectrum = jnp.fft.rfft(signal.astype(jnp.float32).T, n=size_fft, axis=1)
        grad_prod = jnp.fft.irfft(jnp.conj(filt_spectrum) * sig_spectrum, n=size_fft, axis=1)[:, :LENGTH]
        grad_prod = grad_prod.T.astype(jnp.bfloat16).astype(jnp.float32)
        grad_key = (grad_prod * value_seq.astype(jnp.float32)).astype(jnp.bfloat16)
        grad_value = (grad_prod * key_seq.astype(jnp.float32)).astype(jnp.bfloat16)
        filt_term = jnp.fft.irfft(jnp.conj(prod_spectrum) * sig_spectrum, n=size_fft, axis=1)[:, :LENGTH]
        return (grad_key, grad_value, filt_term.astype(jnp.float32))
    grad_key, grad_value, filt_terms = lax.map(one_sequence, (grad_out, query_proj, key_proj, value_proj))
    grad_query = (grad_out.astype(jnp.float32) * conv_out.astype(jnp.float32)).astype(jnp.bfloat16)
    filter_grad = lax.optimization_barrier(jnp.sum(filt_terms, axis=0)) * (1.0 / math.sqrt(BATCH * LENGTH))
    return (grad_query, grad_key, grad_value, filter_grad)
```

```python
import functools
import math

import jax
import jax.numpy as jnp
import ml_dtypes
import numpy as np
from jax import lax
from jax.experimental import pallas as pl
from jax.experimental.pallas import tpu as pltpu
from jax.sharding import PartitionSpec as P

MESH = pl.DeviceIdType.MESH
BF = jnp.bfloat16
F32 = jnp.float32

ROWS = 128
BLOCKS = 64
OWN = 16
SEQS = 4
ZS = 8
PLANE = 32
SIZE = 2 * ROWS * BLOCKS


def split(table):
    high = table.astype(ml_dtypes.bfloat16)
    low = (table - high.astype(np.float64)).astype(ml_dtypes.bfloat16)
    return high, low


def make_tables():
    half = np.arange(BLOCKS) + 0.5
    rows = np.arange(ROWS)
    slot = np.arange(BLOCKS)
    zh, plane = slot // PLANE, slot % PLANE
    arrived = (plane // 2) * 4 + zh * 2 + plane % 2
    out = {}
    for name, blocks in (("d", arrived), ("f", slot)):
        angle = 2 * np.pi * half[:, None] * blocks[None, :] / (2 * BLOCKS)
        first = np.concatenate([np.cos(angle), -np.sin(angle)], axis=0)
        high, low = split(first)
        out["e" + name] = np.concatenate([high, low] if name == "d" else [high, high, low], axis=1)
        high, low = split(first.T * (2.0 / SIZE))
        out["i" + name] = np.concatenate([high, low], axis=1)
    angle = 2 * np.pi * half[:, None] * rows[None, :] / SIZE
    out["wc"] = np.tile(np.cos(angle), (1, 2)).astype(np.float32)
    out["ws"] = np.tile(np.sin(angle), (1, 2)).astype(np.float32)
    angle = 2 * np.pi * rows[:, None] * rows[None, :] / ROWS
    cos, sin = np.cos(angle), np.sin(angle)
    out["dh"], out["dl"] = split(np.block([[cos, -sin], [sin, cos]]))
    out["bh"], out["bl"] = split(np.block([[cos, sin], [-sin, cos]]))
    return out


NAMES = ("ed", "ef", "id", "if", "wc", "ws", "dh", "dl", "bh", "bl")


def dot(a, b):
    return jnp.dot(a, b, preferred_element_type=F32)


def body(*refs):
    (g_h, q_h, k_h, v_h, c_h, f_h) = refs[:6]
    tables_h = refs[6 : 6 + len(NAMES)]
    gq_h, gk_h, gv_h, fg_h = refs[16:20]
    (g, q, k, v, co, filt, *tables) = refs[20 : 27 - 1 + len(NAMES)]
    ed, ef, idt, ift, wc, ws, dh, dl, bh, bl = tables
    (
        gq, gk, gv, fgo,
        zs_s, zs_p, zr_s, zr_p, pr_s, pr_p,
        gout, rp, gt,
        spec, fspec, acc, xs, zb, fgs, fgr,
        in_sem, out_sem, self_sem,
        zsend, zrecv, psend, precv, fsend, frecv,
    ) = refs[26 + len(NAMES) :]

    dp = lax.axis_index("dp")
    seq = lax.axis_index("seq")
    zh = (seq // 2) % 2
    z = zh * 4 + dp
    py, px, pc = seq // 16, (seq // 4) % 4, seq % 2
    w_me = dp * 2 + zh
    q_me = py * 8 + px * 2 + pc

    def z_peer(step):
        other = (z + step) % ZS
        return (other % 4, py * 16 + px * 4 + (other // 4) * 2 + pc), (other % 4) * 2 + other // 4

    def plane_peer(step):
        y, x, c = (py + step // 8) % 4, (px + (step // 2) % 4) % 4, (pc + step % 2) % 2
        return (dp, y * 16 + x * 4 + zh * 2 + c), y * 8 + x * 2 + c

    pairs = [(g_h.at[0], g), (q_h.at[0], q), (k_h.at[0], k), (v_h.at[0], v), (c_h.at[0], co)]
    pairs.append((f_h.at[pl.ds(dp * OWN, OWN), :], filt))
    pairs += list(zip(tables_h, tables))
    loads = [pltpu.make_async_copy(a, b, in_sem.at[n]) for n, (a, b) in enumerate(pairs)]
    for copy in loads:
        copy.start()

    barrier = pltpu.get_barrier_semaphore()

    @pl.loop(1, ZS)
    def _(step):
        pl.semaphore_signal(barrier, inc=1, device_id=z_peer(step)[0], device_id_type=MESH)

    @pl.loop(1, PLANE)
    def _(step):
        pl.semaphore_signal(barrier, inc=1, device_id=plane_peer(step)[0], device_id_type=MESH)

    def turn(left, right, out):
        @pl.loop(0, 32)
        def _(m):
            lanes = pl.ds(pl.multiple_of(m * 128, 128), 128)
            value = left[:, lanes].astype(F32) * right[:, lanes].astype(F32)
            tiles = value.T.astype(BF)
            for t in range(8):
                out[(t % 4) * 2 + m % 2, (m // 2) * 2 + t // 4] = tiles[t * OWN : (t + 1) * OWN]

    def z_start(n, src, dst):
        @pl.loop(1, ZS)
        def _(step):
            device, slot = z_peer(step)
            pltpu.make_async_remote_copy(
                src_ref=src.at[slot], dst_ref=dst.at[w_me], send_sem=zsend.at[n], recv_sem=zrecv.at[n],
                device_id=device, device_id_type=MESH,
            ).start()
        pltpu.make_async_copy(src.at[w_me], dst.at[w_me], self_sem.at[n]).start()

    def z_wait_send(n, src):
        pltpu.make_async_copy(src.at[pl.ds(0, ZS - 1)], src.at[pl.ds(0, ZS - 1)], zsend.at[n]).wait()

    def z_wait_recv(n, src, dst):
        pltpu.make_async_copy(src.at[w_me], dst.at[w_me], self_sem.at[n]).wait()
        pltpu.make_async_copy(dst.at[pl.ds(0, ZS - 1)], dst.at[pl.ds(0, ZS - 1)], zrecv.at[n]).wait()

    def plane_start(n, src, dst):
        @pl.loop(1, PLANE)
        def _(step):
            device, slot = plane_peer(step)
            pltpu.make_async_remote_copy(
                src_ref=src.at[:, slot], dst_ref=dst.at[:, q_me], send_sem=psend.at[n], recv_sem=precv.at[n],
                device_id=device, device_id_type=MESH,
            ).start()
        pltpu.make_async_copy(src.at[:, q_me], dst.at[:, q_me], self_sem.at[3 + n]).start()

    def plane_wait_send(n, src):
        part = src.at[:, pl.ds(0, PLANE - 1)]
        pltpu.make_async_copy(part, part, psend.at[n]).wait()

    def plane_wait_recv(n, src, dst):
        pltpu.make_async_copy(src.at[:, q_me], dst.at[:, q_me], self_sem.at[3 + n]).wait()
        part = dst.at[:, pl.ds(0, PLANE - 1)]
        pltpu.make_async_copy(part, part, precv.at[n]).wait()

    def channel(i):
        return xs[pl.ds(i, BLOCKS, stride=OWN), :]

    def second(rows, high, low):
        data = zb[rows, :]
        return dot(data, high[...]) + dot(data, low[...])

    def forward_first(exact):
        for pair in range(0, OWN, 2):
            x = jnp.concatenate([channel(pair), channel(pair + 1)], axis=1)
            if exact:
                x = x.astype(BF)
                y = dot(ed[...], jnp.concatenate([x, x], axis=0))
            else:
                high = x.astype(BF)
                low = (x - high.astype(F32)).astype(BF)
                y = dot(ef[...], jnp.concatenate([high, low, high], axis=0))
            re, im = y[:BLOCKS], y[BLOCKS:]
            turned_re = re * wc[...] + im * ws[...]
            turned_im = im * wc[...] - re * ws[...]
            for j in range(2):
                lanes = slice(j * ROWS, (j + 1) * ROWS)
                value = jnp.concatenate([turned_re[:, lanes], turned_im[:, lanes]], axis=1)
                zb[(pair + j) * BLOCKS : (pair + j + 1) * BLOCKS, :] = value.astype(BF)

    def inverse(chunk, table):
        inner = second(slice(chunk * 256, (chunk + 1) * 256), bh, bl)
        for pair in range(0, 4, 2):
            parts = []
            for j in (pair, pair + 1):
                re, im = inner[j * BLOCKS : (j + 1) * BLOCKS, :ROWS], inner[j * BLOCKS : (j + 1) * BLOCKS, ROWS:]
                cos, sin = wc[:, :ROWS], ws[:, :ROWS]
                parts.append(jnp.concatenate([re * cos - im * sin, im * cos + re * sin], axis=0).astype(BF))
            both = jnp.concatenate(parts, axis=1)
            y = dot(table[...], jnp.concatenate([both, both], axis=0))
            for j in range(2):
                xs[pl.ds(chunk * 4 + pair + j, BLOCKS, stride=OWN), :] = y[:, j * ROWS : (j + 1) * ROWS]

    loads[0].wait()
    loads[1].wait()
    turn(g, q, zs_s)
    pl.semaphore_wait(barrier, ZS - 1 + PLANE - 1)
    z_start(0, zs_s, zr_s)
    loads[2].wait()
    loads[3].wait()
    turn(k, v, zs_p)

    loads[4].wait()

    @pl.loop(0, 32)
    def _(m):
        lanes = pl.ds(pl.multiple_of(m * 128, 128), 128)
        gq[:, lanes] = (g[:, lanes].astype(F32) * co[:, lanes].astype(F32)).astype(BF)

    gq_out = pltpu.make_async_copy(gq, gq_h.at[0], out_sem.at[0])
    gq_out.start()

    for copy in loads[5:]:
        copy.wait()

    @pl.loop(0, BLOCKS)
    def _(a):
        rows = pl.ds(pl.multiple_of(a * OWN, OWN), OWN)
        xs[rows, :] = filt[:, pl.ds(pl.multiple_of(a * ROWS, ROWS), ROWS)]

    forward_first(False)
    for chunk in range(4):
        rows = slice(chunk * 256, (chunk + 1) * 256)
        fspec[rows, :] = second(rows, dh, dl)

    z_wait_send(0, zs_s)
    z_start(1, zs_p, zr_p)
    z_wait_recv(0, zs_s, zr_s)
    plane_start(0, zr_s, pr_s)
    plane_wait_recv(0, zr_s, pr_s)

    @pl.loop(0, SEQS)
    def _(b):
        xs[...] = pr_s[pl.ds(b * 2, 2)].astype(F32).reshape(BLOCKS * OWN, ROWS)
        forward_first(True)
        for chunk in range(4):
            rows = slice(chunk * 256, (chunk + 1) * 256)
            s = second(rows, dh, dl)
            spec[b, rows, :] = s
            s_re, s_im = s[:, :ROWS], s[:, ROWS:]
            f_re, f_im = fspec[rows, :ROWS], fspec[rows, ROWS:]
            value = jnp.concatenate([f_re * s_re + f_im * s_im, f_re * s_im - f_im * s_re], axis=1)
            zb[rows, :] = value.astype(BF)
            inverse(chunk, idt)
        gout[pl.ds(b * 2, 2)] = xs[...].astype(BF).reshape(2, PLANE, OWN, ROWS)

    plane_start(2, gout, rp)
    z_wait_recv(1, zs_p, zr_p)
    plane_start(1, zr_p, pr_p)
    plane_wait_recv(2, gout, rp)
    z_start(2, rp, gt)
    plane_wait_recv(1, zr_p, pr_p)

    @pl.loop(0, SEQS)
    def _(b):
        xs[...] = pr_p[pl.ds(b * 2, 2)].astype(F32).reshape(BLOCKS * OWN, ROWS)
        forward_first(True)
        for chunk in range(4):
            rows = slice(chunk * 256, (chunk + 1) * 256)
            p = second(rows, dh, dl)
            p_re, p_im = p[:, :ROWS], p[:, ROWS:]
            s_re, s_im = spec[b, rows, :ROWS], spec[b, rows, ROWS:]
            value = jnp.concatenate([p_re * s_re + p_im * s_im, p_re * s_im - p_im * s_re], axis=1)
            acc[rows, :] = jnp.where(b == 0, value, acc[rows, :] + value)

    zb[...] = acc[...].astype(BF)
    for chunk in range(4):
        inverse(chunk, ift)

    @pl.loop(0, BLOCKS)
    def _(a):
        rows = pl.ds(pl.multiple_of(a * OWN, OWN), OWN)
        fgs[a // 16, :, pl.ds(pl.multiple_of((a % 16) * ROWS, ROWS), ROWS)] = xs[rows, :].astype(BF)

    @pl.loop(1, SEQS)
    def _(step):
        other = (dp + step) % SEQS
        pltpu.make_async_remote_copy(
            src_ref=fgs.at[other], dst_ref=fgr.at[dp], send_sem=fsend, recv_sem=frecv,
            device_id=(other, seq), device_id_type=MESH,
        ).start()

    fgr[dp] = fgs[dp]

    z_wait_recv(2, rp, gt)

    @pl.loop(0, 32)
    def _(m):
        lanes = pl.ds(pl.multiple_of(m * 128, 128), 128)
        tiles = [gt[(t % 4) * 2 + m % 2, (m // 2) * 2 + t // 4] for t in range(8)]
        value = jnp.concatenate(tiles, axis=0).astype(F32).T
        gk[:, lanes] = (value * v[:, lanes].astype(F32)).astype(BF)
        gv[:, lanes] = (value * k[:, lanes].astype(F32)).astype(BF)

    outs = [
        pltpu.make_async_copy(gk, gk_h.at[0], out_sem.at[1]),
        pltpu.make_async_copy(gv, gv_h.at[0], out_sem.at[2]),
    ]
    for copy in outs:
        copy.start()

    pltpu.make_async_copy(fgr.at[pl.ds(0, SEQS - 1)], fgr.at[pl.ds(0, SEQS - 1)], frecv).wait()
    scale = 1.0 / math.sqrt(SEQS * ROWS * BLOCKS)
    for d in range(SEQS):
        fgo[d * OWN : (d + 1) * OWN, :] = fgr[d].astype(F32) * scale
    outs.append(pltpu.make_async_copy(fgo, fg_h, out_sem.at[3]))
    outs[-1].start()

    z_wait_send(1, zs_p)
    z_wait_send(2, rp)
    plane_wait_send(0, zr_s)
    plane_wait_send(1, zr_p)
    plane_wait_send(2, gout)
    pltpu.make_async_copy(fgs.at[pl.ds(0, SEQS - 1)], fgs.at[pl.ds(0, SEQS - 1)], fsend).wait()
    gq_out.wait()
    for copy in outs:
        copy.wait()


def local(grad_out, query_proj, key_proj, value_proj, conv_out, filters):
    tables = make_tables()
    values = [jnp.asarray(tables[name]) for name in NAMES]
    rows, channels = grad_out.shape[1:]
    wide = pltpu.VMEM((rows, channels), BF)
    moved = pltpu.VMEM((ZS, PLANE, OWN, ROWS), BF)
    any_spec = pl.BlockSpec(memory_space=pl.ANY)
    dma = pltpu.SemaphoreType.DMA
    return pl.pallas_call(
        body,
        out_shape=[jax.ShapeDtypeStruct(grad_out.shape, BF)] * 3
        + [jax.ShapeDtypeStruct((SEQS * OWN, filters.shape[1] // SEQS), F32)],
        in_specs=[any_spec] * (6 + len(NAMES)),
        out_specs=[any_spec] * 4,
        scratch_shapes=[wide] * 5
        + [pltpu.VMEM((OWN, filters.shape[1]), F32)]
        + [pltpu.VMEM(a.shape, a.dtype) for a in values]
        + [wide] * 3
        + [pltpu.VMEM((SEQS * OWN, filters.shape[1] // SEQS), F32)]
        + [moved] * 9
        + [
            pltpu.VMEM((SEQS, OWN * BLOCKS, 2 * ROWS), F32),
            pltpu.VMEM((OWN * BLOCKS, 2 * ROWS), F32),
            pltpu.VMEM((OWN * BLOCKS, 2 * ROWS), F32),
            pltpu.VMEM((OWN * BLOCKS, ROWS), F32),
            pltpu.VMEM((OWN * BLOCKS, 2 * ROWS), BF),
            pltpu.VMEM((SEQS, OWN, filters.shape[1] // SEQS), BF),
            pltpu.VMEM((SEQS, OWN, filters.shape[1] // SEQS), BF),
            dma((6 + len(NAMES),)),
            dma((4,)),
            dma((6,)),
            dma((3,)),
            dma((3,)),
            dma((3,)),
            dma((3,)),
            dma(()),
            dma(()),
        ],
        compiler_params=pltpu.CompilerParams(
            collective_id=0, has_side_effects=True, vmem_limit_bytes=56 * 1024 * 1024
        ),
    )(grad_out, query_proj, key_proj, value_proj, conv_out, filters, *values)


def solution(mesh):
    across = P("dp", "seq", None)
    return jax.shard_map(
        local,
        mesh=mesh,
        in_specs=(across,) * 5 + (P("seq", None),),
        out_specs=(across,) * 3 + (P("seq", "dp"),),
        check_vma=False,
    )
```

```python
import functools
import math

import jax
import jax.numpy as jnp
import ml_dtypes
import numpy as np
from jax import lax
from jax.experimental import pallas as pl
from jax.experimental.pallas import tpu as pltpu
from jax.sharding import PartitionSpec as P

MESH = pl.DeviceIdType.MESH
BF = jnp.bfloat16
F32 = jnp.float32

ROWS = 128
BLOCKS = 64
OWN = 16
SEQS = 4
ZS = 8
PLANE = 32
SIZE = 2 * ROWS * BLOCKS


def split(table):
    high = table.astype(ml_dtypes.bfloat16)
    low = (table - high.astype(np.float64)).astype(ml_dtypes.bfloat16)
    return high, low


def make_tables():
    half = np.arange(BLOCKS) + 0.5
    rows = np.arange(ROWS)
    slot = np.arange(BLOCKS)
    zh, plane = slot // PLANE, slot % PLANE
    arrived = (plane // 2) * 4 + zh * 2 + plane % 2
    out = {}
    for name, blocks in (("d", arrived), ("f", slot)):
        angle = 2 * np.pi * half[:, None] * blocks[None, :] / (2 * BLOCKS)
        first = np.concatenate([np.cos(angle), -np.sin(angle)], axis=0)
        high, low = split(first)
        out["e" + name] = np.concatenate([high, low] if name == "d" else [high, high, low], axis=1)
        high, low = split(first.T * (2.0 / SIZE))
        out["i" + name] = np.concatenate([high, high, low], axis=1)
    angle = 2 * np.pi * half[:, None] * rows[None, :] / SIZE
    out["wc"] = np.tile(np.cos(angle), (1, 2)).astype(np.float32)
    out["ws"] = np.tile(np.sin(angle), (1, 2)).astype(np.float32)
    angle = 2 * np.pi * rows[:, None] * rows[None, :] / ROWS
    cos, sin = np.cos(angle), np.sin(angle)
    out["dh"], out["dl"] = split(np.block([[cos, -sin], [sin, cos]]))
    out["bh"], out["bl"] = split(np.block([[cos, sin], [-sin, cos]]))
    return out


NAMES = ("ed", "ef", "id", "if", "wc", "ws", "dh", "dl", "bh", "bl")


def dot(a, b):
    return jnp.dot(a, b, preferred_element_type=F32)


def parts(value):
    high = value.astype(BF)
    return high, (value - high.astype(F32)).astype(BF)


def body(*refs):
    (g_h, q_h, k_h, v_h, f_h) = refs[:5]
    tables_h = refs[5 : 5 + len(NAMES)]
    gt, fgr = refs[15:17]
    (g, q, k, v, filt, *tables) = refs[17 : 22 + len(NAMES)]
    ed, ef, idt, ift, wc, ws, dh, dl, bh, bl = tables
    (
        sent_s, sent_p, got_s, got_p, gout,
        spec, fspec, acc, xs, zh_b, zl_b, fgs,
        in_sem, self_sem, gate, send, recv, fsend, frecv,
    ) = refs[22 + len(NAMES) :]

    dp = lax.axis_index("dp")
    seq = lax.axis_index("seq")
    z = (seq // 2) % 2 * 4 + dp
    py, px, pc = seq // 16, (seq // 4) % 4, seq % 2

    column = []
    for step in range(ZS):
        other = (z + step) % ZS
        column.append((other % 4, (other // 4) * 2, ((other % 4) * 2 + other // 4) * PLANE))
    me = column[0][2] + py * 8 + px * 2 + pc

    def in_plane(step):
        y, x, c = (py + step // 8) % 4, (px + (step // 2) % 4) % 4, (pc + step % 2) % 2
        return y * 16 + x * 4 + c, y * 8 + x * 2 + c

    pairs = [(g_h.at[0], g), (q_h.at[0], q), (k_h.at[0], k), (v_h.at[0], v)]
    pairs.append((f_h.at[pl.ds(dp * OWN, OWN), :], filt))
    pairs += list(zip(tables_h, tables))
    loads = [pltpu.make_async_copy(a, b, in_sem.at[n]) for n, (a, b) in enumerate(pairs)]
    for copy in loads:
        copy.start()

    barrier = pltpu.get_barrier_semaphore()
    for dpi, add, _ in column[1:]:
        device = (dpi, py * 16 + px * 4 + pc + add)
        pl.semaphore_signal(barrier, inc=1, device_id=device, device_id_type=MESH)

    @pl.loop(1, PLANE)
    def _(step):
        device = (dp, in_plane(step)[0] + column[0][1])
        pl.semaphore_signal(barrier, inc=1, device_id=device, device_id_type=MESH)

    def turn(left, right, out):
        @pl.loop(0, 32)
        def _(m):
            lanes = pl.ds(pl.multiple_of(m * 128, 128), 128)
            value = left[:, lanes].astype(F32) * right[:, lanes].astype(F32)
            tiles = value.T.astype(BF)
            for t in range(8):
                out[((t % 4) * 2 + m % 2) * PLANE + (m // 2) * 2 + t // 4] = tiles[t * OWN : (t + 1) * OWN]

    def exchange(n, src, dst):
        def one(entry, base, slot):
            pltpu.make_async_remote_copy(
                src_ref=src.at[entry[2] + slot], dst_ref=dst.at[me], send_sem=send.at[n], recv_sem=recv.at[n],
                device_id=(entry[0], base + entry[1]), device_id_type=MESH,
            ).start()

        base, slot = in_plane(0)
        for entry in column[1:]:
            one(entry, base, slot)
        pltpu.make_async_copy(src.at[me], dst.at[me], self_sem.at[n]).start()

        @pl.loop(1, PLANE)
        def _(step):
            base, slot = in_plane(step)
            for entry in column:
                one(entry, base, slot)

    def sent(n, src):
        part = src.at[pl.ds(0, ZS * PLANE - 1)]
        pltpu.make_async_copy(part, part, send.at[n]).wait()

    def arrived(n, src, dst):
        pltpu.make_async_copy(src.at[me], dst.at[me], self_sem.at[n]).wait()
        part = dst.at[pl.ds(0, ZS * PLANE - 1)]
        pltpu.make_async_copy(part, part, recv.at[n]).wait()

    def channel(i):
        return xs[pl.ds(i, BLOCKS, stride=OWN), :]

    def store(rows, value):
        zh_b[rows, :], zl_b[rows, :] = parts(value)

    def second(rows, high, low):
        return dot(zh_b[rows, :], high[...]) + dot(zl_b[rows, :], high[...]) + dot(zh_b[rows, :], low[...])

    def forward_first(exact):
        for pair in range(0, OWN, 2):
            x = jnp.concatenate([channel(pair), channel(pair + 1)], axis=1)
            if exact:
                x = x.astype(BF)
                y = dot(ed[...], jnp.concatenate([x, x], axis=0))
            else:
                high, low = parts(x)
                y = dot(ef[...], jnp.concatenate([high, low, high], axis=0))
            re, im = y[:BLOCKS], y[BLOCKS:]
            turned_re = re * wc[...] + im * ws[...]
            turned_im = im * wc[...] - re * ws[...]
            for j in range(2):
                lanes = slice(j * ROWS, (j + 1) * ROWS)
                value = jnp.concatenate([turned_re[:, lanes], turned_im[:, lanes]], axis=1)
                store(slice((pair + j) * BLOCKS, (pair + j + 1) * BLOCKS), value)

    def inverse(chunk, table):
        inner = second(slice(chunk * 256, (chunk + 1) * 256), bh, bl)
        for pair in range(0, 4, 2):
            both = []
            for j in (pair, pair + 1):
                re, im = inner[j * BLOCKS : (j + 1) * BLOCKS, :ROWS], inner[j * BLOCKS : (j + 1) * BLOCKS, ROWS:]
                cos, sin = wc[:, :ROWS], ws[:, :ROWS]
                both.append(jnp.concatenate([re * cos - im * sin, im * cos + re * sin], axis=0))
            high, low = parts(jnp.concatenate(both, axis=1))
            y = dot(table[...], jnp.concatenate([high, low, high], axis=0))
            for j in range(2):
                xs[pl.ds(chunk * 4 + pair + j, BLOCKS, stride=OWN), :] = y[:, j * ROWS : (j + 1) * ROWS]

    loads[0].wait()
    loads[1].wait()
    turn(g, q, sent_s)
    pl.semaphore_wait(barrier, ZS - 1 + PLANE - 1)
    for dpi, add, _ in column[1:]:
        device = (dpi, py * 16 + px * 4 + pc + add)
        pl.semaphore_signal(gate, inc=1, device_id=device, device_id_type=MESH)
    pl.semaphore_wait(gate, ZS - 1)
    exchange(0, sent_s, got_s)
    loads[2].wait()
    loads[3].wait()
    turn(k, v, sent_p)

    for copy in loads[4:]:
        copy.wait()

    @pl.loop(0, BLOCKS)
    def _(a):
        rows = pl.ds(pl.multiple_of(a * OWN, OWN), OWN)
        xs[rows, :] = filt[:, pl.ds(pl.multiple_of(a * ROWS, ROWS), ROWS)]

    forward_first(False)
    for chunk in range(4):
        rows = slice(chunk * 256, (chunk + 1) * 256)
        fspec[rows, :] = second(rows, dh, dl)

    sent(0, sent_s)
    exchange(1, sent_p, got_p)
    arrived(0, sent_s, got_s)

    @pl.loop(0, SEQS)
    def _(b):
        tiles = pl.ds(b * BLOCKS, BLOCKS)
        xs[...] = got_s[tiles].astype(F32).reshape(BLOCKS * OWN, ROWS)
        forward_first(True)
        for chunk in range(4):
            rows = slice(chunk * 256, (chunk + 1) * 256)
            s = second(rows, dh, dl)
            spec[b, rows, :] = s
            s_re, s_im = s[:, :ROWS], s[:, ROWS:]
            f_re, f_im = fspec[rows, :ROWS], fspec[rows, ROWS:]
            store(rows, jnp.concatenate([f_re * s_re + f_im * s_im, f_re * s_im - f_im * s_re], axis=1))
            inverse(chunk, idt)
        gout[tiles] = xs[...].astype(BF).reshape(BLOCKS, OWN, ROWS)

    exchange(2, gout, gt)
    arrived(1, sent_p, got_p)

    @pl.loop(0, SEQS)
    def _(b):
        xs[...] = got_p[pl.ds(b * BLOCKS, BLOCKS)].astype(F32).reshape(BLOCKS * OWN, ROWS)
        forward_first(True)
        for chunk in range(4):
            rows = slice(chunk * 256, (chunk + 1) * 256)
            p = second(rows, dh, dl)
            p_re, p_im = p[:, :ROWS], p[:, ROWS:]
            s_re, s_im = spec[b, rows, :ROWS], spec[b, rows, ROWS:]
            value = jnp.concatenate([p_re * s_re + p_im * s_im, p_re * s_im - p_im * s_re], axis=1)
            acc[rows, :] = jnp.where(b == 0, value, acc[rows, :] + value)

    for chunk in range(4):
        rows = slice(chunk * 256, (chunk + 1) * 256)
        store(rows, acc[rows, :])
        inverse(chunk, ift)

    @pl.loop(0, BLOCKS)
    def _(a):
        rows = pl.ds(pl.multiple_of(a * OWN, OWN), OWN)
        fgs[a // 16, :, pl.ds(pl.multiple_of((a % 16) * ROWS, ROWS), ROWS)] = xs[rows, :].astype(BF)

    for step in range(1, SEQS):
        other = (dp + step) % SEQS
        pltpu.make_async_remote_copy(
            src_ref=fgs.at[other], dst_ref=fgr.at[dp], send_sem=fsend, recv_sem=frecv,
            device_id=(other, seq), device_id_type=MESH,
        ).start()
    own = pltpu.make_async_copy(fgs.at[dp], fgr.at[dp], self_sem.at[3])
    own.start()

    sent(1, sent_p)
    sent(2, gout)
    arrived(2, gout, gt)
    own.wait()
    pltpu.make_async_copy(fgr.at[pl.ds(0, SEQS - 1)], fgr.at[pl.ds(0, SEQS - 1)], frecv).wait()
    pltpu.make_async_copy(fgs.at[pl.ds(0, SEQS - 1)], fgs.at[pl.ds(0, SEQS - 1)], fsend).wait()


def finish(g, k, v, co, gt, fgr, gq, gk, gv, fg):
    gq[0] = (g[0].astype(F32) * co[0].astype(F32)).astype(BF)
    for m in range(gt.shape[2] * 2):
        lanes = slice(m * 128, (m + 1) * 128)
        tiles = [gt[t % 4, m % 2, m // 2, t // 4] for t in range(8)]
        value = jnp.concatenate(tiles, axis=0).astype(F32).T
        gk[0, :, lanes] = (value * v[0, :, lanes].astype(F32)).astype(BF)
        gv[0, :, lanes] = (value * k[0, :, lanes].astype(F32)).astype(BF)
    fg[...] = fgr[...].astype(F32).reshape(fg.shape) * (1.0 / math.sqrt(SEQS * ROWS * BLOCKS))


def local(grad_out, query_proj, key_proj, value_proj, conv_out, filters):
    tables = make_tables()
    values = [jnp.asarray(tables[name]) for name in NAMES]
    rows, channels = grad_out.shape[1:]
    taps = filters.shape[1] // SEQS
    wide = pltpu.VMEM((rows, channels), BF)
    moved = pltpu.VMEM((ZS * PLANE, OWN, ROWS), BF)
    any_spec = pl.BlockSpec(memory_space=pl.ANY)
    dma = pltpu.SemaphoreType.DMA
    gt, fgr = pl.pallas_call(
        body,
        out_shape=[
            jax.ShapeDtypeStruct((ZS * PLANE, OWN, ROWS), BF),
            jax.ShapeDtypeStruct((SEQS, OWN, taps), BF),
        ],
        in_specs=[any_spec] * (5 + len(NAMES)),
        out_specs=[any_spec] * 2,
        scratch_shapes=[wide] * 4
        + [pltpu.VMEM((OWN, filters.shape[1]), F32)]
        + [pltpu.VMEM(a.shape, a.dtype) for a in values]
        + [moved] * 5
        + [
            pltpu.VMEM((SEQS, OWN * BLOCKS, 2 * ROWS), F32),
            pltpu.VMEM((OWN * BLOCKS, 2 * ROWS), F32),
            pltpu.VMEM((OWN * BLOCKS, 2 * ROWS), F32),
            pltpu.VMEM((OWN * BLOCKS, ROWS), F32),
            pltpu.VMEM((OWN * BLOCKS, 2 * ROWS), BF),
            pltpu.VMEM((OWN * BLOCKS, 2 * ROWS), BF),
            pltpu.VMEM((SEQS, OWN, taps), BF),
            dma((5 + len(NAMES),)),
            dma((4,)),
            pltpu.SemaphoreType.REGULAR,
            dma((3,)),
            dma((3,)),
            dma(()),
            dma(()),
        ],
        compiler_params=pltpu.CompilerParams(
            collective_id=0, has_side_effects=True, vmem_limit_bytes=56 * 1024 * 1024
        ),
    )(grad_out, query_proj, key_proj, value_proj, filters, *values)

    steps = 4
    block = pl.BlockSpec((1, rows, channels // steps), lambda i: (0, 0, i))
    return pl.pallas_call(
        finish,
        grid=(steps,),
        out_shape=[jax.ShapeDtypeStruct(grad_out.shape, BF)] * 3
        + [jax.ShapeDtypeStruct((SEQS * OWN, taps), F32)],
        in_specs=[block] * 4
        + [
            pl.BlockSpec((4, 2, 16 // steps, 2, OWN, ROWS), lambda i: (0, 0, i, 0, 0, 0)),
            pl.BlockSpec((SEQS, OWN, taps // steps), lambda i: (0, 0, i)),
        ],
        out_specs=[block] * 3 + [pl.BlockSpec((SEQS * OWN, taps // steps), lambda i: (0, i))],
        compiler_params=pltpu.CompilerParams(vmem_limit_bytes=32 * 1024 * 1024),
    )(grad_out, key_proj, value_proj, conv_out, gt.reshape(4, 2, 16, 2, OWN, ROWS), fgr)


def solution(mesh):
    across = P("dp", "seq", None)
    return jax.shard_map(
        local,
        mesh=mesh,
        in_specs=(across,) * 5 + (P("seq", None),),
        out_specs=(across,) * 3 + (P("seq", "dp"),),
        check_vma=False,
    )
```

```python
import functools
import math

import jax
import jax.numpy as jnp
import ml_dtypes
import numpy as np
from jax import lax
from jax.experimental import pallas as pl
from jax.experimental.pallas import tpu as pltpu
from jax.sharding import PartitionSpec as P

MESH = pl.DeviceIdType.MESH
BF = jnp.bfloat16
F32 = jnp.float32

ROWS = 128
BLOCKS = 64
OWN = 16
SEQS = 4
ZS = 8
PLANE = 32
SIZE = 2 * ROWS * BLOCKS


def split(table):
    high = table.astype(ml_dtypes.bfloat16)
    low = (table - high.astype(np.float64)).astype(ml_dtypes.bfloat16)
    return high, low


def make_tables():
    half = np.arange(BLOCKS) + 0.5
    rows = np.arange(ROWS)
    slot = np.arange(BLOCKS)
    zh, plane = slot // PLANE, slot % PLANE
    arrived = (plane // 2) * 4 + zh * 2 + plane % 2
    out = {}
    for name, blocks in (("d", arrived), ("f", slot)):
        angle = 2 * np.pi * half[:, None] * blocks[None, :] / (2 * BLOCKS)
        first = np.concatenate([np.cos(angle), -np.sin(angle)], axis=0)
        high, low = split(first)
        out["e" + name] = np.concatenate([high, low] if name == "d" else [high, high, low], axis=1)
        high, low = split(first.T * (2.0 / SIZE))
        out["i" + name] = np.concatenate([high, high, low], axis=1)
    angle = 2 * np.pi * half[:, None] * rows[None, :] / SIZE
    out["wc"] = np.tile(np.cos(angle), (1, 2)).astype(np.float32)
    out["ws"] = np.tile(np.sin(angle), (1, 2)).astype(np.float32)
    angle = 2 * np.pi * rows[:, None] * rows[None, :] / ROWS
    cos, sin = np.cos(angle), np.sin(angle)
    out["dh"], out["dl"] = split(np.block([[cos, -sin], [sin, cos]]))
    out["bh"], out["bl"] = split(np.block([[cos, sin], [-sin, cos]]))
    return out


NAMES = ("ed", "ef", "id", "if", "wc", "ws", "dh", "dl", "bh", "bl")


def dot(a, b):
    return jnp.dot(a, b, preferred_element_type=F32)


def parts(value):
    high = value.astype(BF)
    return high, (value - high.astype(F32)).astype(BF)


def body(*refs):
    (g_h, q_h, k_h, v_h, c_h, f_h) = refs[:6]
    tables_h = refs[6 : 6 + len(NAMES)]
    gq, gk, gv, fg = refs[16:20]
    (g, q, k, v, co, filt, *tables) = refs[20 : 26 + len(NAMES)]
    ed, ef, idt, ift, wc, ws, dh, dl, bh, bl = tables
    (
        sent_s, sent_p, got_s, got_p, gout, gt, mid,
        spec, fspec, acc, xs, zh_b, zl_b, fgs, fgr,
        first_sem, in_sem, self_sem, gate, send, recv, back, fsend, frecv, msend, mrecv, hsend, hrecv,
    ) = refs[26 + len(NAMES) :]

    dp = lax.axis_index("dp")
    seq = lax.axis_index("seq")
    z = (seq // 2) % 2 * 4 + dp
    py, px, pc = seq // 16, (seq // 4) % 4, seq % 2

    column = []
    for step in range(ZS):
        other = (z + step) % ZS
        column.append((other % 4, (other // 4) * 2, ((other % 4) * 2 + other // 4) * PLANE))
    me = column[0][2] + py * 8 + px * 2 + pc

    def in_plane(step):
        y, x, c = (py + step // 8) % 4, (px + (step // 2) % 4) % 4, (pc + step % 2) % 2
        return y * 16 + x * 4 + c, y * 8 + x * 2 + c

    first = []
    for part in range(4):
        lanes = pl.ds(pl.multiple_of((py + part) % 4 * 1024, 1024), 1024)
        for n, (a, b) in enumerate(((g_h, g), (q_h, q))):
            first.append(pltpu.make_async_copy(a.at[0, :, lanes], b.at[:, lanes], first_sem.at[part * 2 + n]))
    for copy in first:
        copy.start()

    barrier = pltpu.get_barrier_semaphore()
    for dpi, add, _ in column[1:]:
        device = (dpi, py * 16 + px * 4 + pc + add)
        pl.semaphore_signal(barrier, inc=1, device_id=device, device_id_type=MESH)

    @pl.loop(1, PLANE)
    def _(step):
        device = (dp, in_plane(step)[0] + column[0][1])
        pl.semaphore_signal(barrier, inc=1, device_id=device, device_id_type=MESH)

    pairs = [(k_h.at[0], k), (v_h.at[0], v), (c_h.at[0], co)]
    pairs.append((f_h.at[pl.ds(dp * OWN, OWN), :], filt))
    pairs += list(zip(tables_h, tables))
    loads = [pltpu.make_async_copy(a, b, in_sem.at[n]) for n, (a, b) in enumerate(pairs)]
    for copy in loads:
        copy.start()

    def turn(left, right, out, m):
        lanes = pl.ds(pl.multiple_of(m * 128, 128), 128)
        value = left[:, lanes].astype(F32) * right[:, lanes].astype(F32)
        tiles = value.T.astype(BF)
        for t in range(8):
            out[((t % 4) * 2 + m % 2) * PLANE + (m // 2) * 2 + t // 4] = tiles[t * OWN : (t + 1) * OWN]

    def tile(src, dst, send_sem, recv_sem, entry, place):
        base, slot = place
        pltpu.make_async_remote_copy(
            src_ref=src.at[entry[2] + slot], dst_ref=dst.at[me], send_sem=send_sem, recv_sem=recv_sem,
            device_id=(entry[0], base + entry[1]), device_id_type=MESH,
        ).start()

    def exchange(n, src, dst, recv_sem):
        for entry in column[1:]:
            tile(src, dst, send.at[n], recv_sem(0), entry, in_plane(0))
        pltpu.make_async_copy(src.at[me], dst.at[me], self_sem.at[n]).start()

        @pl.loop(1, PLANE)
        def _(step):
            place = in_plane(step)
            for entry in column:
                tile(src, dst, send.at[n], recv_sem(step), entry, place)

    def sent(n, src, count=ZS * PLANE - 1):
        part = src.at[pl.ds(0, count)]
        pltpu.make_async_copy(part, part, send.at[n]).wait()

    def arrived(n, dst, count):
        part = dst.at[pl.ds(0, count)]
        pltpu.make_async_copy(part, part, recv.at[n]).wait()

    def channel(i):
        return xs[pl.ds(i, BLOCKS, stride=OWN), :]

    def store(rows, value):
        zh_b[rows, :], zl_b[rows, :] = parts(value)

    def second(rows, high, low):
        return dot(zh_b[rows, :], high[...]) + dot(zl_b[rows, :], high[...]) + dot(zh_b[rows, :], low[...])

    def forward_first(exact):
        for pair in range(0, OWN, 2):
            x = jnp.concatenate([channel(pair), channel(pair + 1)], axis=1)
            if exact:
                x = x.astype(BF)
                y = dot(ed[...], jnp.concatenate([x, x], axis=0))
            else:
                high, low = parts(x)
                y = dot(ef[...], jnp.concatenate([high, low, high], axis=0))
            re, im = y[:BLOCKS], y[BLOCKS:]
            turned_re = re * wc[...] + im * ws[...]
            turned_im = im * wc[...] - re * ws[...]
            for j in range(2):
                lanes = slice(j * ROWS, (j + 1) * ROWS)
                value = jnp.concatenate([turned_re[:, lanes], turned_im[:, lanes]], axis=1)
                store(slice((pair + j) * BLOCKS, (pair + j + 1) * BLOCKS), value)

    def inverse(chunk, table):
        inner = second(slice(chunk * 256, (chunk + 1) * 256), bh, bl)
        for pair in range(0, 4, 2):
            both = []
            for j in (pair, pair + 1):
                re, im = inner[j * BLOCKS : (j + 1) * BLOCKS, :ROWS], inner[j * BLOCKS : (j + 1) * BLOCKS, ROWS:]
                cos, sin = wc[:, :ROWS], ws[:, :ROWS]
                both.append(jnp.concatenate([re * cos - im * sin, im * cos + re * sin], axis=0))
            high, low = parts(jnp.concatenate(both, axis=1))
            y = dot(table[...], jnp.concatenate([high, low, high], axis=0))
            for j in range(2):
                xs[pl.ds(chunk * 4 + pair + j, BLOCKS, stride=OWN), :] = y[:, j * ROWS : (j + 1) * ROWS]

    def turn_signal(part):
        first[2 * part].wait()
        first[2 * part + 1].wait()

        @pl.loop(0, 8)
        def _(i):
            turn(g, q, sent_s, (py + part) % 4 * 8 + i)

    def signal_tiles(begin, end):
        @pl.loop(begin, end)
        def _(step):
            place = in_plane(step)
            for entry in column:
                tile(sent_s, got_s, send.at[0], recv.at[0], entry, place)

    turn_signal(0)
    pl.semaphore_wait(barrier, ZS - 1 + PLANE - 1)
    for dpi, add, _ in column[1:]:
        device = (dpi, py * 16 + px * 4 + pc + add)
        pl.semaphore_signal(gate, inc=1, device_id=device, device_id_type=MESH)
    row = py * 8
    q_me = row + px * 2 + pc
    mine = pl.ds(column[0][2] // 4, 8)
    for dpi, add, slot in column[1:]:
        pltpu.make_async_remote_copy(
            src_ref=sent_s.at[pl.ds(slot + row, 8)], dst_ref=mid.at[mine], send_sem=msend, recv_sem=mrecv,
            device_id=(dpi, py * 16 + px * 4 + pc + add), device_id_type=MESH,
        ).start()
    own_mid = pltpu.make_async_copy(sent_s.at[pl.ds(column[0][2] + row, 8)], mid.at[mine], self_sem.at[0])
    own_mid.start()
    for part in range(1, 4):
        turn_signal(part)
    loads[0].wait()
    loads[1].wait()

    @pl.loop(0, 32)
    def _(m):
        turn(k, v, sent_p, m)

    pl.semaphore_wait(gate, ZS - 1)
    signal_tiles(8, 20)
    own_mid.wait()
    pltpu.make_async_copy(mid.at[pl.ds(0, 56)], mid.at[pl.ds(0, 56)], mrecv).wait()
    by_source = mid.reshape(ZS, 8, OWN, ROWS)
    got_by_source = got_s.reshape(ZS, PLANE, OWN, ROWS)

    @pl.loop(1, 8)
    def _(step):
        base, slot = in_plane(step)
        pltpu.make_async_remote_copy(
            src_ref=by_source.at[:, slot - row], dst_ref=got_by_source.at[:, q_me], send_sem=hsend, recv_sem=hrecv,
            device_id=(dp, base + column[0][1]), device_id_type=MESH,
        ).start()

    own_row = pltpu.make_async_copy(by_source.at[:, px * 2 + pc], got_by_source.at[:, q_me], self_sem.at[4])
    own_row.start()
    signal_tiles(20, PLANE)

    for copy in loads[2:]:
        copy.wait()

    @pl.loop(0, BLOCKS)
    def _(a):
        rows = pl.ds(pl.multiple_of(a * OWN, OWN), OWN)
        xs[rows, :] = filt[:, pl.ds(pl.multiple_of(a * ROWS, ROWS), ROWS)]

    forward_first(False)
    for chunk in range(4):
        rows = slice(chunk * 256, (chunk + 1) * 256)
        fspec[rows, :] = second(rows, dh, dl)

    sent(0, sent_s, 192)
    exchange(1, sent_p, got_p, lambda step: recv.at[1])

    @pl.loop(0, 32)
    def _(m):
        lanes = pl.ds(pl.multiple_of(m * 128, 128), 128)
        gq[0, :, lanes] = (g[:, lanes].astype(F32) * co[:, lanes].astype(F32)).astype(BF)

    own_row.wait()
    arrived(0, got_s, 192)
    pltpu.make_async_copy(got_s.at[pl.ds(0, 56)], got_s.at[pl.ds(0, 56)], hrecv).wait()

    @pl.loop(0, SEQS)
    def _(b):
        tiles = pl.ds(b * BLOCKS, BLOCKS)
        xs[...] = got_s[tiles].astype(F32).reshape(BLOCKS * OWN, ROWS)
        forward_first(True)
        for chunk in range(4):
            rows = slice(chunk * 256, (chunk + 1) * 256)
            s = second(rows, dh, dl)
            spec[b, rows, :] = s
            s_re, s_im = s[:, :ROWS], s[:, ROWS:]
            f_re, f_im = fspec[rows, :ROWS], fspec[rows, ROWS:]
            store(rows, jnp.concatenate([f_re * s_re + f_im * s_im, f_re * s_im - f_im * s_re], axis=1))
            inverse(chunk, idt)
        gout[tiles] = xs[...].astype(BF).reshape(BLOCKS, OWN, ROWS)

    exchange(2, gout, gt, lambda step: back.at[step // 8])
    pltpu.make_async_copy(sent_p.at[me], got_p.at[me], self_sem.at[1]).wait()
    arrived(1, got_p, ZS * PLANE - 1)

    @pl.loop(0, SEQS)
    def _(b):
        xs[...] = got_p[pl.ds(b * BLOCKS, BLOCKS)].astype(F32).reshape(BLOCKS * OWN, ROWS)
        forward_first(True)
        for chunk in range(4):
            rows = slice(chunk * 256, (chunk + 1) * 256)
            p = second(rows, dh, dl)
            p_re, p_im = p[:, :ROWS], p[:, ROWS:]
            s_re, s_im = spec[b, rows, :ROWS], spec[b, rows, ROWS:]
            value = jnp.concatenate([p_re * s_re + p_im * s_im, p_re * s_im - p_im * s_re], axis=1)
            acc[rows, :] = jnp.where(b == 0, value, acc[rows, :] + value)

    for chunk in range(4):
        rows = slice(chunk * 256, (chunk + 1) * 256)
        store(rows, acc[rows, :])
        inverse(chunk, ift)

    @pl.loop(0, BLOCKS)
    def _(a):
        rows = pl.ds(pl.multiple_of(a * OWN, OWN), OWN)
        fgs[a // 16, :, pl.ds(pl.multiple_of((a % 16) * ROWS, ROWS), ROWS)] = xs[rows, :].astype(BF)

    for step in range(1, SEQS):
        other = (dp + step) % SEQS
        pltpu.make_async_remote_copy(
            src_ref=fgs.at[other], dst_ref=fgr.at[dp], send_sem=fsend, recv_sem=frecv,
            device_id=(other, seq), device_id_type=MESH,
        ).start()
    own = pltpu.make_async_copy(fgs.at[dp], fgr.at[dp], self_sem.at[3])
    own.start()

    sent(1, sent_p)
    sent(2, gout)
    pltpu.make_async_copy(sent_s.at[pl.ds(0, 56)], sent_s.at[pl.ds(0, 56)], msend).wait()
    pltpu.make_async_copy(mid.at[pl.ds(0, 56)], mid.at[pl.ds(0, 56)], hsend).wait()

    pltpu.make_async_copy(gout.at[me], gt.at[me], self_sem.at[2]).wait()
    for part in range(4):
        count = ZS * 8 - (part == 0)
        pltpu.make_async_copy(gt.at[pl.ds(0, count)], gt.at[pl.ds(0, count)], back.at[part]).wait()

        @pl.loop(0, 8)
        def _(i):
            m = (py + 4 - part) % 4 * 8 + i
            lanes = pl.ds(pl.multiple_of(m * 128, 128), 128)
            tiles = [gt[((t % 4) * 2 + m % 2) * PLANE + (m // 2) * 2 + t // 4] for t in range(8)]
            value = jnp.concatenate(tiles, axis=0).astype(F32).T
            gk[0, :, lanes] = (value * v[:, lanes].astype(F32)).astype(BF)
            gv[0, :, lanes] = (value * k[:, lanes].astype(F32)).astype(BF)

    own.wait()
    pltpu.make_async_copy(fgr.at[pl.ds(0, SEQS - 1)], fgr.at[pl.ds(0, SEQS - 1)], frecv).wait()
    pltpu.make_async_copy(fgs.at[pl.ds(0, SEQS - 1)], fgs.at[pl.ds(0, SEQS - 1)], fsend).wait()
    for d in range(SEQS):
        fg[d * OWN : (d + 1) * OWN, :] = fgr[d].astype(F32) * (1.0 / math.sqrt(SEQS * ROWS * BLOCKS))


def copy_out(*refs):
    copies = [pltpu.make_async_copy(refs[n], refs[4 + n], refs[8].at[n]) for n in range(4)]
    for copy in copies:
        copy.start()
    for copy in copies:
        copy.wait()


def local(grad_out, query_proj, key_proj, value_proj, conv_out, filters):
    tables = make_tables()
    values = [jnp.asarray(tables[name]) for name in NAMES]
    rows, channels = grad_out.shape[1:]
    taps = filters.shape[1] // SEQS
    wide = pltpu.VMEM((rows, channels), BF)
    moved = pltpu.VMEM((ZS * PLANE, OWN, ROWS), BF)
    any_spec = pl.BlockSpec(memory_space=pl.ANY)
    dma = pltpu.SemaphoreType.DMA
    arrays = (grad_out, query_proj, key_proj, value_proj, conv_out, filters, *values)
    held = pl.pallas_call(
        body,
        out_shape=[pltpu.VMEM(grad_out.shape, BF)] * 3 + [pltpu.VMEM((SEQS * OWN, taps), F32)],
        in_specs=[any_spec] * (6 + len(NAMES)),
        out_specs=[pl.BlockSpec(memory_space=pltpu.VMEM)] * 4,
        scratch_shapes=[wide] * 5
        + [pltpu.VMEM((OWN, filters.shape[1]), F32)]
        + [pltpu.VMEM(a.shape, a.dtype) for a in values]
        + [moved] * 6
        + [pltpu.VMEM((ZS * 8, OWN, ROWS), BF)]
        + [
            pltpu.VMEM((SEQS, OWN * BLOCKS, 2 * ROWS), F32),
            pltpu.VMEM((OWN * BLOCKS, 2 * ROWS), F32),
            pltpu.VMEM((OWN * BLOCKS, 2 * ROWS), F32),
            pltpu.VMEM((OWN * BLOCKS, ROWS), F32),
            pltpu.VMEM((OWN * BLOCKS, 2 * ROWS), BF),
            pltpu.VMEM((OWN * BLOCKS, 2 * ROWS), BF),
            pltpu.VMEM((SEQS, OWN, taps), BF),
            pltpu.VMEM((SEQS, OWN, taps), BF),
            dma((8,)),
            dma((4 + len(NAMES),)),
            dma((5,)),
            pltpu.SemaphoreType.REGULAR,
            dma((3,)),
            dma((2,)),
            dma((4,)),
            *[dma(())] * 6,
        ],
        compiler_params=pltpu.CompilerParams(
            collective_id=0, has_side_effects=True, vmem_limit_bytes=44 * 1024 * 1024
        ),
    )(*[pltpu.with_memory_space_constraint(x, pltpu.HBM) for x in arrays])
    return pl.pallas_call(
        copy_out,
        out_shape=[jax.ShapeDtypeStruct(x.shape, x.dtype) for x in held],
        in_specs=[pl.BlockSpec(memory_space=pltpu.VMEM)] * 4,
        out_specs=[any_spec] * 4,
        scratch_shapes=[dma((4,))],
        compiler_params=pltpu.CompilerParams(vmem_limit_bytes=16 * 1024 * 1024),
    )(*[pltpu.with_memory_space_constraint(x, pltpu.VMEM) for x in held])


def solution(mesh):
    across = P("dp", "seq", None)
    return jax.shard_map(
        local,
        mesh=mesh,
        in_specs=(across,) * 5 + (P("seq", None),),
        out_specs=(across,) * 3 + (P("seq", "dp"),),
        check_vma=False,
    )
```

```python
import functools
import math

import jax
import jax.numpy as jnp
import ml_dtypes
import numpy as np
from jax import lax
from jax.experimental import pallas as pl
from jax.experimental.pallas import tpu as pltpu
from jax.sharding import PartitionSpec as P

MESH = pl.DeviceIdType.MESH
BF = jnp.bfloat16
F32 = jnp.float32

ROWS = 128
BLOCKS = 64
OWN = 16
SEQS = 4
ZS = 8
PLANE = 32
SIZE = 2 * ROWS * BLOCKS


def split(table):
    high = table.astype(ml_dtypes.bfloat16)
    low = (table - high.astype(np.float64)).astype(ml_dtypes.bfloat16)
    return high, low


def make_tables():
    half = np.arange(BLOCKS) + 0.5
    rows = np.arange(ROWS)
    slot = np.arange(BLOCKS)
    zh, plane = slot // PLANE, slot % PLANE
    arrived = (plane // 2) * 4 + zh * 2 + plane % 2
    out = {}
    for name, blocks in (("d", arrived), ("f", slot)):
        angle = 2 * np.pi * half[:, None] * blocks[None, :] / (2 * BLOCKS)
        first = np.concatenate([np.cos(angle), -np.sin(angle)], axis=0)
        high, low = split(first)
        out["e" + name] = np.concatenate([high, low] if name == "d" else [high, high, low], axis=1)
        high, low = split(first.T * (2.0 / SIZE))
        out["i" + name] = np.concatenate([high, high, low], axis=1)
    angle = 2 * np.pi * half[:, None] * rows[None, :] / SIZE
    out["wc"] = np.tile(np.cos(angle), (1, 2)).astype(np.float32)
    out["ws"] = np.tile(np.sin(angle), (1, 2)).astype(np.float32)
    angle = 2 * np.pi * rows[:, None] * rows[None, :] / ROWS
    cos, sin = np.cos(angle), np.sin(angle)
    out["dh"], out["dl"] = split(np.block([[cos, -sin], [sin, cos]]))
    out["bh"], out["bl"] = split(np.block([[cos, sin], [-sin, cos]]))
    return out


NAMES = ("ed", "ef", "id", "if", "wc", "ws", "dh", "dl", "bh", "bl")


def dot(a, b):
    return jnp.dot(a, b, preferred_element_type=F32)


def parts(value):
    high = value.astype(BF)
    return high, (value - high.astype(F32)).astype(BF)


def body(*refs):
    (g_h, q_h, k_h, v_h, c_h, f_h) = refs[:6]
    tables_h = refs[6 : 6 + len(NAMES)]
    gq, gk, gv, fg = refs[16:20]
    (g, q, k, v, co, filt, *tables) = refs[20 : 26 + len(NAMES)]
    ed, ef, idt, ift, wc, ws, dh, dl, bh, bl = tables
    (
        sent_s, sent_p, got_s, got_p, gout, gt, mid,
        spec, fspec, acc, xs, zh_b, zl_b, fgs, fgr,
        first_sem, in_sem, self_sem, gate, send, recv, back, fsend, frecv, msend, mrecv, hsend, hrecv,
    ) = refs[26 + len(NAMES) :]

    dp = lax.axis_index("dp")
    seq = lax.axis_index("seq")
    z = (seq // 2) % 2 * 4 + dp
    py, px, pc = seq // 16, (seq // 4) % 4, seq % 2

    column = []
    for step in range(ZS):
        other = (z + step) % ZS
        column.append((other % 4, (other // 4) * 2, ((other % 4) * 2 + other // 4) * PLANE))
    me = column[0][2] + py * 8 + px * 2 + pc

    def in_plane(step):
        y, x, c = (py + step // 8) % 4, (px + (step // 2) % 4) % 4, (pc + step % 2) % 2
        return y * 16 + x * 4 + c, y * 8 + x * 2 + c

    barrier = pltpu.get_barrier_semaphore()
    for dpi, add, _ in column[1:]:
        device = (dpi, py * 16 + px * 4 + pc + add)
        pl.semaphore_signal(barrier, inc=1, device_id=device, device_id_type=MESH)

    first = []
    for part in range(4):
        lanes = pl.ds(pl.multiple_of((py + part) % 4 * 1024, 1024), 1024)
        for n, (a, b) in enumerate(((g_h, g), (q_h, q))):
            first.append(pltpu.make_async_copy(a.at[0, :, lanes], b.at[:, lanes], first_sem.at[part * 2 + n]))
    for copy in first:
        copy.start()

    along_y = [(py + step) % 4 * 16 + column[0][1] for step in range(4)]
    along_x = [(px + step) % 4 * 4 for step in range(4)]
    cores = [pc, (pc + 1) % 2]
    for step in range(1, PLANE):
        device = (dp, along_y[step // 8] + (along_x[step // 2 % 4] + cores[step % 2]))
        pl.semaphore_signal(barrier, inc=1, device_id=device, device_id_type=MESH)

    def turn(left, right, out, m):
        lanes = pl.ds(pl.multiple_of(m * 128, 128), 128)
        value = left[:, lanes].astype(F32) * right[:, lanes].astype(F32)
        tiles = value.T.astype(BF)
        for t in range(8):
            out[((t % 4) * 2 + m % 2) * PLANE + (m // 2) * 2 + t // 4] = tiles[t * OWN : (t + 1) * OWN]

    def tile(src, dst, send_sem, recv_sem, entry, place):
        base, slot = place
        pltpu.make_async_remote_copy(
            src_ref=src.at[entry[2] + slot], dst_ref=dst.at[me], send_sem=send_sem, recv_sem=recv_sem,
            device_id=(entry[0], base + entry[1]), device_id_type=MESH,
        ).start()

    def exchange(n, src, dst, recv_sem):
        for entry in column[1:]:
            tile(src, dst, send.at[n], recv_sem(0), entry, in_plane(0))
        pltpu.make_async_copy(src.at[me], dst.at[me], self_sem.at[n]).start()

        @pl.loop(1, PLANE)
        def _(step):
            place = in_plane(step)
            for entry in column:
                tile(src, dst, send.at[n], recv_sem(step), entry, place)

    def sent(n, src, count=ZS * PLANE - 1):
        part = src.at[pl.ds(0, count)]
        pltpu.make_async_copy(part, part, send.at[n]).wait()

    def arrived(n, dst, count):
        part = dst.at[pl.ds(0, count)]
        pltpu.make_async_copy(part, part, recv.at[n]).wait()

    def channel(i):
        return xs[pl.ds(i, BLOCKS, stride=OWN), :]

    def store(rows, value):
        zh_b[rows, :], zl_b[rows, :] = parts(value)

    def second(rows, high, low):
        return dot(zh_b[rows, :], high[...]) + dot(zl_b[rows, :], high[...]) + dot(zh_b[rows, :], low[...])

    def forward_first(exact):
        for pair in range(0, OWN, 2):
            x = jnp.concatenate([channel(pair), channel(pair + 1)], axis=1)
            if exact:
                x = x.astype(BF)
                y = dot(ed[...], jnp.concatenate([x, x], axis=0))
            else:
                high, low = parts(x)
                y = dot(ef[...], jnp.concatenate([high, low, high], axis=0))
            re, im = y[:BLOCKS], y[BLOCKS:]
            turned_re = re * wc[...] + im * ws[...]
            turned_im = im * wc[...] - re * ws[...]
            for j in range(2):
                lanes = slice(j * ROWS, (j + 1) * ROWS)
                value = jnp.concatenate([turned_re[:, lanes], turned_im[:, lanes]], axis=1)
                store(slice((pair + j) * BLOCKS, (pair + j + 1) * BLOCKS), value)

    def inverse(chunk, table):
        inner = second(slice(chunk * 256, (chunk + 1) * 256), bh, bl)
        for pair in range(0, 4, 2):
            both = []
            for j in (pair, pair + 1):
                re, im = inner[j * BLOCKS : (j + 1) * BLOCKS, :ROWS], inner[j * BLOCKS : (j + 1) * BLOCKS, ROWS:]
                cos, sin = wc[:, :ROWS], ws[:, :ROWS]
                both.append(jnp.concatenate([re * cos - im * sin, im * cos + re * sin], axis=0))
            high, low = parts(jnp.concatenate(both, axis=1))
            y = dot(table[...], jnp.concatenate([high, low, high], axis=0))
            for j in range(2):
                xs[pl.ds(chunk * 4 + pair + j, BLOCKS, stride=OWN), :] = y[:, j * ROWS : (j + 1) * ROWS]

    def turn_signal(part):
        first[2 * part].wait()
        first[2 * part + 1].wait()

        @pl.loop(0, 8)
        def _(i):
            turn(g, q, sent_s, (py + part) % 4 * 8 + i)

    def signal_tiles(begin, end):
        @pl.loop(begin, end)
        def _(step):
            place = in_plane(step)
            for entry in column:
                tile(sent_s, got_s, send.at[0], recv.at[0], entry, place)

    turn_signal(0)
    pl.semaphore_wait(barrier, ZS - 1 + PLANE - 1)
    for dpi, add, _ in column[1:]:
        device = (dpi, py * 16 + px * 4 + pc + add)
        pl.semaphore_signal(gate, inc=1, device_id=device, device_id_type=MESH)
    row = py * 8
    q_me = row + px * 2 + pc
    mine = pl.ds(column[0][2] // 4, 8)
    for dpi, add, slot in column[1:]:
        pltpu.make_async_remote_copy(
            src_ref=sent_s.at[pl.ds(slot + row, 8)], dst_ref=mid.at[mine], send_sem=msend, recv_sem=mrecv,
            device_id=(dpi, py * 16 + px * 4 + pc + add), device_id_type=MESH,
        ).start()
    own_mid = pltpu.make_async_copy(sent_s.at[pl.ds(column[0][2] + row, 8)], mid.at[mine], self_sem.at[0])
    own_mid.start()
    pairs = [(k_h.at[0], k), (v_h.at[0], v), (c_h.at[0], co)]
    pairs.append((f_h.at[pl.ds(dp * OWN, OWN), :], filt))
    pairs += list(zip(tables_h, tables))
    loads = [pltpu.make_async_copy(a, b, in_sem.at[n]) for n, (a, b) in enumerate(pairs)]
    for copy in loads:
        copy.start()

    for part in range(1, 4):
        turn_signal(part)
    loads[0].wait()
    loads[1].wait()

    @pl.loop(0, 32)
    def _(m):
        turn(k, v, sent_p, m)

    pl.semaphore_wait(gate, ZS - 1)
    signal_tiles(8, 20)
    own_mid.wait()
    pltpu.make_async_copy(mid.at[pl.ds(0, 56)], mid.at[pl.ds(0, 56)], mrecv).wait()
    by_source = mid.reshape(ZS, 8, OWN, ROWS)
    got_by_source = got_s.reshape(ZS, PLANE, OWN, ROWS)

    @pl.loop(1, 8)
    def _(step):
        base, slot = in_plane(step)
        pltpu.make_async_remote_copy(
            src_ref=by_source.at[:, slot - row], dst_ref=got_by_source.at[:, q_me], send_sem=hsend, recv_sem=hrecv,
            device_id=(dp, base + column[0][1]), device_id_type=MESH,
        ).start()

    own_row = pltpu.make_async_copy(by_source.at[:, px * 2 + pc], got_by_source.at[:, q_me], self_sem.at[4])
    own_row.start()
    signal_tiles(20, PLANE)

    for copy in loads[2:]:
        copy.wait()

    @pl.loop(0, BLOCKS)
    def _(a):
        rows = pl.ds(pl.multiple_of(a * OWN, OWN), OWN)
        xs[rows, :] = filt[:, pl.ds(pl.multiple_of(a * ROWS, ROWS), ROWS)]

    forward_first(False)
    for chunk in range(4):
        rows = slice(chunk * 256, (chunk + 1) * 256)
        fspec[rows, :] = second(rows, dh, dl)

    sent(0, sent_s, 192)
    exchange(1, sent_p, got_p, lambda step: recv.at[1])

    @pl.loop(0, 32)
    def _(m):
        lanes = pl.ds(pl.multiple_of(m * 128, 128), 128)
        gq[0, :, lanes] = (g[:, lanes].astype(F32) * co[:, lanes].astype(F32)).astype(BF)

    own_row.wait()
    arrived(0, got_s, 192)
    pltpu.make_async_copy(got_s.at[pl.ds(0, 56)], got_s.at[pl.ds(0, 56)], hrecv).wait()

    @pl.loop(0, SEQS)
    def _(b):
        tiles = pl.ds(b * BLOCKS, BLOCKS)
        xs[...] = got_s[tiles].astype(F32).reshape(BLOCKS * OWN, ROWS)
        forward_first(True)
        for chunk in range(4):
            rows = slice(chunk * 256, (chunk + 1) * 256)
            s = second(rows, dh, dl)
            spec[b, rows, :] = s
            s_re, s_im = s[:, :ROWS], s[:, ROWS:]
            f_re, f_im = fspec[rows, :ROWS], fspec[rows, ROWS:]
            store(rows, jnp.concatenate([f_re * s_re + f_im * s_im, f_re * s_im - f_im * s_re], axis=1))
            inverse(chunk, idt)
        gout[tiles] = xs[...].astype(BF).reshape(BLOCKS, OWN, ROWS)

    def return_tiles(begin, end, entries):
        @pl.loop(begin, end)
        def _(step):
            place = in_plane(step)
            for entry in entries:
                tile(gout, gt, send.at[2], back.at[step // 4], entry, place)

    for entry in column[1:]:
        tile(gout, gt, send.at[2], back.at[0], entry, in_plane(0))
    pltpu.make_async_copy(gout.at[me], gt.at[me], self_sem.at[2]).start()
    return_tiles(1, 20, column)
    for half in range(2):
        return_tiles(20, PLANE, [(w, half * 2, (w * 2 + half) * PLANE) for w in range(4)])

    pltpu.make_async_copy(sent_p.at[me], got_p.at[me], self_sem.at[1]).wait()
    arrived(1, got_p, ZS * PLANE - 1)

    @pl.loop(0, SEQS)
    def _(b):
        xs[...] = got_p[pl.ds(b * BLOCKS, BLOCKS)].astype(F32).reshape(BLOCKS * OWN, ROWS)
        forward_first(True)
        for chunk in range(4):
            rows = slice(chunk * 256, (chunk + 1) * 256)
            p = second(rows, dh, dl)
            p_re, p_im = p[:, :ROWS], p[:, ROWS:]
            s_re, s_im = spec[b, rows, :ROWS], spec[b, rows, ROWS:]
            value = jnp.concatenate([p_re * s_re + p_im * s_im, p_re * s_im - p_im * s_re], axis=1)
            acc[rows, :] = jnp.where(b == 0, value, acc[rows, :] + value)

    for chunk in range(4):
        rows = slice(chunk * 256, (chunk + 1) * 256)
        store(rows, acc[rows, :])
        inverse(chunk, ift)

    @pl.loop(0, BLOCKS)
    def _(a):
        rows = pl.ds(pl.multiple_of(a * OWN, OWN), OWN)
        fgs[a // 16, :, pl.ds(pl.multiple_of((a % 16) * ROWS, ROWS), ROWS)] = xs[rows, :].astype(BF)

    for step in range(1, SEQS):
        other = (dp + step) % SEQS
        pltpu.make_async_remote_copy(
            src_ref=fgs.at[other], dst_ref=fgr.at[dp], send_sem=fsend, recv_sem=frecv,
            device_id=(other, seq), device_id_type=MESH,
        ).start()
    own = pltpu.make_async_copy(fgs.at[dp], fgr.at[dp], self_sem.at[3])
    own.start()

    sent(1, sent_p)
    sent(2, gout)
    pltpu.make_async_copy(sent_s.at[pl.ds(0, 56)], sent_s.at[pl.ds(0, 56)], msend).wait()
    pltpu.make_async_copy(mid.at[pl.ds(0, 56)], mid.at[pl.ds(0, 56)], hsend).wait()

    pltpu.make_async_copy(gout.at[me], gt.at[me], self_sem.at[2]).wait()
    for part in range(8):
        if part == 7:
            own.wait()
            pltpu.make_async_copy(fgr.at[pl.ds(0, SEQS - 1)], fgr.at[pl.ds(0, SEQS - 1)], frecv).wait()
            pltpu.make_async_copy(fgs.at[pl.ds(0, SEQS - 1)], fgs.at[pl.ds(0, SEQS - 1)], fsend).wait()
            for d in range(SEQS):
                fg[d * OWN : (d + 1) * OWN, :] = fgr[d].astype(F32) * (1.0 / math.sqrt(SEQS * ROWS * BLOCKS))

        count = ZS * 4 - (part == 0)
        pltpu.make_async_copy(gt.at[pl.ds(0, count)], gt.at[pl.ds(0, count)], back.at[part]).wait()

        @pl.loop(0, 4)
        def _(i):
            m = ((py + 4 - part // 2) % 4 * 4 + (px + 8 - part % 2 * 2 - i // 2) % 4) * 2 + i % 2
            lanes = pl.ds(pl.multiple_of(m * 128, 128), 128)
            tiles = [gt[((t % 4) * 2 + m % 2) * PLANE + (m // 2) * 2 + t // 4] for t in range(8)]
            value = jnp.concatenate(tiles, axis=0).astype(F32).T
            gk[0, :, lanes] = (value * v[:, lanes].astype(F32)).astype(BF)
            gv[0, :, lanes] = (value * k[:, lanes].astype(F32)).astype(BF)


def copy_out(*refs):
    copies = []
    for n in range(4):
        rows = refs[n].shape[-2] // 4
        for part in range(4):
            span = (0,) * (n < 3) + (pl.ds(part * rows, rows),)
            copies.append(pltpu.make_async_copy(refs[n].at[span], refs[4 + n].at[span], refs[8].at[n, part]))
    for copy in copies:
        copy.start()
    for copy in copies:
        copy.wait()


def local(grad_out, query_proj, key_proj, value_proj, conv_out, filters):
    tables = make_tables()
    values = [jnp.asarray(tables[name]) for name in NAMES]
    rows, channels = grad_out.shape[1:]
    taps = filters.shape[1] // SEQS
    wide = pltpu.VMEM((rows, channels), BF)
    moved = pltpu.VMEM((ZS * PLANE, OWN, ROWS), BF)
    any_spec = pl.BlockSpec(memory_space=pl.ANY)
    dma = pltpu.SemaphoreType.DMA
    arrays = (grad_out, query_proj, key_proj, value_proj, conv_out, filters, *values)
    held = pl.pallas_call(
        body,
        out_shape=[pltpu.VMEM(grad_out.shape, BF)] * 3 + [pltpu.VMEM((SEQS * OWN, taps), F32)],
        in_specs=[any_spec] * (6 + len(NAMES)),
        out_specs=[pl.BlockSpec(memory_space=pltpu.VMEM)] * 4,
        scratch_shapes=[wide] * 5
        + [pltpu.VMEM((OWN, filters.shape[1]), F32)]
        + [pltpu.VMEM(a.shape, a.dtype) for a in values]
        + [moved] * 6
        + [pltpu.VMEM((ZS * 8, OWN, ROWS), BF)]
        + [
            pltpu.VMEM((SEQS, OWN * BLOCKS, 2 * ROWS), F32),
            pltpu.VMEM((OWN * BLOCKS, 2 * ROWS), F32),
            pltpu.VMEM((OWN * BLOCKS, 2 * ROWS), F32),
            pltpu.VMEM((OWN * BLOCKS, ROWS), F32),
            pltpu.VMEM((OWN * BLOCKS, 2 * ROWS), BF),
            pltpu.VMEM((OWN * BLOCKS, 2 * ROWS), BF),
            pltpu.VMEM((SEQS, OWN, taps), BF),
            pltpu.VMEM((SEQS, OWN, taps), BF),
            dma((8,)),
            dma((4 + len(NAMES),)),
            dma((5,)),
            pltpu.SemaphoreType.REGULAR,
            dma((3,)),
            dma((2,)),
            dma((8,)),
            *[dma(())] * 6,
        ],
        compiler_params=pltpu.CompilerParams(
            collective_id=0, has_side_effects=True, vmem_limit_bytes=44 * 1024 * 1024
        ),
    )(*[pltpu.with_memory_space_constraint(x, pltpu.HBM) for x in arrays])
    return pl.pallas_call(
        copy_out,
        out_shape=[jax.ShapeDtypeStruct(x.shape, x.dtype) for x in held],
        in_specs=[pl.BlockSpec(memory_space=pltpu.VMEM)] * 4,
        out_specs=[any_spec] * 4,
        scratch_shapes=[dma((4, 4))],
        compiler_params=pltpu.CompilerParams(vmem_limit_bytes=16 * 1024 * 1024),
    )(*[pltpu.with_memory_space_constraint(x, pltpu.VMEM) for x in held])


def solution(mesh):
    across = P("dp", "seq", None)
    return jax.shard_map(
        local,
        mesh=mesh,
        in_specs=(across,) * 5 + (P("seq", None),),
        out_specs=(across,) * 3 + (P("seq", "dp"),),
        check_vma=False,
    )
```
